32 devices in a mesh: row: 2 (over core), col: 4 (over y, x), inner: 4 (over z).
Axes of the slice: x: 2, y: 2, z: 4, core: 2. Of those that a mesh axis runs over, the one named last changes fastest.
Arguments:
- density: bfloat16 [64, 16, 256, 256], P('row', ('col', 'inner')), may hold values from -1.5 to 1.5, as said below
- block_cols: int32 [64, 16], replicated, may hold values from 0 to 63, as said below
- mixing: float32 [3], replicated, may hold values from 0.02 to 1.5, as said below
Outputs:
- purified: bfloat16 [64, 16, 256, 256], P('row', ('col', 'inner'))
The draws below stay inside these ranges and needn't reach their ends.
Inputs may be any that keep to these rules, and one draw needn't show every extreme that they name: Slot g of block row i names a block row of group g (rows g * 4 to g * 4 + 3); within one group of block rows, slot g names each row of group g once. Slot i // 4 of row i names i itself. The pattern is symmetric: row block_cols[i, g] names i in slot i // 4. It is consistent: block_cols[block_cols[i, t], g] == block_cols[i, g] for all i, t, g. `density`: block (i, g) is the transpose of block (block_cols[i, g], i // 4). `mixing`: element 0 lies in 0.5 to 1.5, elements 1 and 2 in 0.02 to 0.05.
All inputs are finite; a program needn't handle non-finite values.
Results may differ from the reference program's by a relative error of at most 0.007.
Values may be sent and summed in bfloat16 or wider, within the bound.
A program may use at most 128 MiB of HBM per device.

```python
import jax
import jax.numpy as jnp
from jax import lax

B = 256
K = 16
GS = 4
NB = 64


def pattern(key):
    base = jax.random.fold_in(key, 101)
    keys = jax.random.split(base, K)
    labels = jax.vmap(lambda item: jax.random.permutation(item, GS))(keys).astype(jnp.int32)
    inverse = jnp.argsort(labels, axis=-1, stable=True).astype(jnp.int32)
    group_second = jnp.arange(K, dtype=jnp.int32)[None, :, None]
    mapping = labels[group_second, inverse[:, None, :]]
    table = group_second * GS + mapping
    return jnp.transpose(table, (0, 2, 1)).reshape(K * GS, K).astype(jnp.int32)


def draw_block_cols(key, part):
    return pattern(key)


def draw_density(key, part):
    block_cols = pattern(key)
    noise_key = jax.random.fold_in(key, 202)
    spread = (B * K) ** (-0.25)
    raw = jnp.clip(jax.random.normal(noise_key, (NB, K, B, B), jnp.float32), -5.0, 5.0) * spread
    rows_all = jnp.arange(NB, dtype=jnp.int32)
    own_group = rows_all // GS
    mirror = raw[block_cols, own_group[:, None]]
    density = (raw + jnp.swapaxes(mirror, -1, -2)) * 0.5 ** 0.5
    return density.astype(jnp.bfloat16)


def draw_mixing(key, part):
    mix_key = jax.random.fold_in(key, 303)
    values = jax.random.uniform(mix_key, (3,), jnp.float32, 0.0, 1.0)
    lowers = jnp.array([0.5, 0.02, 0.02], jnp.float32)
    uppers = jnp.array([1.5, 0.05, 0.05], jnp.float32)
    return lowers + values * (uppers - lowers)


def setup_inputs(seed: int = 0) -> dict:
    seeds = jax.random.split(jax.random.key(seed), 4)
    density = draw_density(jax.random.fold_in(seeds[3], 71), 0)
    block_cols = draw_block_cols(jax.random.fold_in(seeds[3], 71), 0)
    mixing = draw_mixing(jax.random.fold_in(seeds[3], 71), 0)
    return dict(density=density, block_cols=block_cols, mixing=mixing)


def multiply(left_blocks, right_blocks, block_cols):
    def one_row(row_number):
        targets = block_cols[row_number]
        gathered = right_blocks[targets].astype(jnp.float32)
        row_left = left_blocks[row_number].astype(jnp.float32)
        return jnp.einsum("tab,tgbc->gac", row_left, gathered, precision=lax.Precision.HIGHEST)
    return lax.map(one_row, jnp.arange(NB, dtype=jnp.int32))


def reference(density, block_cols, mixing):
    square = multiply(density, density, block_cols).astype(jnp.bfloat16)
    rows_all = jnp.arange(NB, dtype=jnp.int32)
    on_diagonal = (block_cols == rows_all[:, None]).astype(jnp.float32)
    identity = jnp.eye(B, dtype=jnp.float32)
    mixer_blocks = (mixing[0] * on_diagonal[:, :, None, None] * identity
                    + mixing[1] * density.astype(jnp.float32)
                    + mixing[2] * square.astype(jnp.float32)).astype(jnp.bfloat16)
    purified = multiply(square, mixer_blocks, block_cols)
    return purified.astype(jnp.bfloat16)
```

```python
import functools

import jax
import jax.numpy as jnp
from jax import lax
from jax.experimental import pallas as pl
from jax.experimental.pallas import tpu as pltpu
from jax.sharding import PartitionSpec as P

GS = 4


def fold_with(panel, piece):
    return jnp.einsum("htab,tgbc->hgac", panel, piece, preferred_element_type=jnp.float32)


def clique_filter(density, block_cols, mixing, row_start):
    row_count = density.shape[0]
    width = density.shape[2]
    groups_here = row_count // GS
    first_group = row_start // GS
    leaders = lax.dynamic_slice_in_dim(block_cols[:GS], first_group, groups_here, 1)
    ordered = density[:, 0][(leaders - row_start).reshape(-1)]
    ordered = ordered.reshape(GS, groups_here, 1, width, width)
    arrived = lax.all_to_all(ordered, "inner", split_axis=0, concat_axis=2, tiled=True)
    blocks = arrived[0]
    slot_count = blocks.shape[1]
    slot_start = lax.axis_index("col") * slot_count
    density_panel = lax.all_gather(blocks, "col", axis=1, tiled=True)
    square = fold_with(density_panel, lax.all_gather(blocks, "row", axis=0, tiled=True)).astype(
        jnp.bfloat16
    )
    group_ids = first_group + jnp.arange(groups_here, dtype=jnp.int32)
    slot_ids = slot_start + jnp.arange(slot_count, dtype=jnp.int32)
    on_diagonal = (group_ids[:, None] == slot_ids[None, :]).astype(jnp.float32)
    identity = jnp.eye(width, dtype=jnp.float32)
    mixer_blocks = (
        mixing[0] * on_diagonal[:, :, None, None] * identity
        + mixing[1] * blocks.astype(jnp.float32)
        + mixing[2] * square.astype(jnp.float32)
    ).astype(jnp.bfloat16)
    square_panel = lax.all_gather(square, "col", axis=1, tiled=True)
    filtered = fold_with(
        square_panel, lax.all_gather(mixer_blocks, "row", axis=0, tiled=True)
    ).astype(jnp.bfloat16)
    returned = lax.all_to_all(filtered[None], "inner", split_axis=2, concat_axis=0, tiled=True)
    regrouped = returned.reshape(GS * groups_here, 1, width, width)
    local_rows = row_start + jnp.arange(row_count, dtype=jnp.int32)
    clique_ids = lax.dynamic_slice_in_dim(block_cols[:, 0], row_start, row_count, 0)
    positions = clique_ids * groups_here + (local_rows // GS - first_group)
    return regrouped[positions]


def product_kernel(
    slots, half, width, mixing_ref, ordered_ref, out_ref,
    left, own, oth, xo, yn, dt, own2, oth2, xo2, yn2, dt2,
    z_send, z_recv, in_sem, send_sems, recv_sems, p_send, p_recv, out_sem,
):
    tile = half // 2
    rows = half * width
    r = lax.axis_index("row")
    c = lax.axis_index("col")
    z = lax.axis_index("inner")
    y, x = c // 2, c % 2
    to_x = {"col": y * 2 + (1 - x)}
    to_y = {"col": (1 - y) * 2 + x}
    to_core = {"row": 1 - r}
    base0 = x * tile
    base1 = (1 - x) * tile
    diag = r == y
    MESH = pl.DeviceIdType.MESH

    def others(k):
        return (z + k) % slots

    barrier = pltpu.get_barrier_semaphore()
    for k in range(1, slots):
        pl.semaphore_signal(barrier, inc=1, device_id={"inner": others(k)}, device_id_type=MESH)
    for target in (to_x, to_y, to_core):
        pl.semaphore_signal(barrier, inc=1, device_id=target, device_id_type=MESH)
    pl.semaphore_wait(barrier, slots - 1 + 3)

    def remote(src, dst, send, recv, target):
        return pltpu.make_async_remote_copy(
            src_ref=src, dst_ref=dst, send_sem=send, recv_sem=recv, device_id=target, device_id_type=MESH
        )

    def z_copy(k):
        to = others(k)
        return remote(ordered_ref.at[to], own.at[z], z_send.at[k], z_recv.at[z], {"inner": to})

    def z_arrival(s):
        return remote(ordered_ref.at[s], own.at[s], z_send.at[0], z_recv.at[s], {"inner": s})

    for k in range(1, slots):
        z_copy(k).start()
    keep = pltpu.make_async_copy(ordered_ref.at[z], own.at[z], in_sem)
    keep.start()

    def links(phase):
        mine, oth_, xo_, yn_, dt_ = ((own, oth, xo, yn, dt), (own2, oth2, xo2, yn2, dt2))[phase]
        diag_rows = pl.ds(pl.multiple_of(base0 * width, width), tile * width)

        def make(kind, index, src, dst, target):
            return lambda s: remote(
                src(s), dst.at[s], send_sems.at[phase, index, s], recv_sems.at[phase, kind, s], target
            )

        return dict(
            core=make(0, 0, lambda s: mine.at[s], oth_, to_core),
            xo=make(1, 1, lambda s: mine.at[s], xo_, to_x),
            yn=make(2, 2, lambda s: mine.at[s], yn_, to_y),
            dt=make(3, 3, lambda s: mine.at[s, diag_rows], dt_, to_x),
            dt_y=make(3, 1, lambda s: dt_.at[s], dt_, to_y),
            xo_relay=make(1, 2, lambda s: xo_.at[s], xo_, to_core),
        )

    def send_first(link, s):
        @pl.when(diag)
        def _():
            link["yn"](s).start()
            link["dt"](s).start()
            link["core"](s).start()

        @pl.when(jnp.logical_not(diag))
        def _():
            link["xo"](s).start()
            link["core"](s).start()

    def wait_sends(link, s):
        @pl.when(diag)
        def _():
            for name in ("yn", "dt", "core", "dt_y"):
                link[name](s).wait_send()

        @pl.when(jnp.logical_not(diag))
        def _():
            for name in ("xo", "core", "xo_relay"):
                link[name](s).wait_send()

    def relay_dt(link, s):
        link["dt"](s).wait_recv()
        link["dt_y"](s).start()

    def relay_xo(link, s):
        link["xo"](s).wait_recv()
        link["xo_relay"](s).start()

    def group(g):
        return pl.ds(pl.multiple_of(g * width, width), width)

    def put_same(source, s):
        def step(g, carry):
            left[base0 + s, group(g), :] = source[s, group(g), :]
            return carry
        lax.fori_loop(0, half, step, 0)

        def flip(g, carry):
            left[base1 + g, group(base0 + s), :] = source[s, group(base1 + g), :].T
            return carry
        lax.fori_loop(0, tile, flip, 0)

    def put_dt(source, s):
        def step(g, carry):
            left[base1 + s, group(base1 + g), :] = source[s, group(g), :]
            return carry
        lax.fori_loop(0, tile, step, 0)

    def put_flipped(source, s, base):
        def step(g, carry):
            left[half + g, group(base + s), :] = source[s, group(g), :].T
            return carry
        lax.fori_loop(0, half, step, 0)

    def put_plain(source, s, base):
        def step(g, carry):
            left[half + base + s, group(g), :] = source[s, group(g), :]
            return carry
        lax.fori_loop(0, half, step, 0)

    chunk = rows // 4

    def multiply(right0, right1, s, row_start):
        here = pl.ds(pl.multiple_of(row_start, chunk), chunk)
        lhs = jnp.concatenate([left[k, here, :] for k in range(2 * half)], axis=1)
        rhs = jnp.concatenate([right0[s], right1[s]], axis=0)
        return jnp.dot(lhs, rhs, preferred_element_type=jnp.float32).astype(jnp.bfloat16)

    link = links(0)
    order = [z, z + 1 - 2 * (z % 2), (z + 2) % 4, 3 - z] if slots == 4 else [others(k) for k in range(slots)]

    def relay_and_put(s):
        @pl.when(diag)
        def _():
            relay_dt(link, s)
            put_same(own, s)
            put_dt(dt, s)
            link["core"](s).wait_recv()
            put_flipped(oth, s, base0)
            link["xo_relay"](s).wait_recv()
            put_flipped(xo, s, base1)

        @pl.when(jnp.logical_not(diag))
        def _():
            relay_xo(link, s)
            put_plain(own, s, base0)
            put_plain(xo, s, base1)
            link["yn"](s).wait_recv()
            put_same(yn, s)
            link["dt_y"](s).wait_recv()
            put_dt(dt, s)
            link["core"](s).wait_recv()

    for k, s in enumerate(order):
        if k == 0:
            keep.wait()
        else:
            z_arrival(s).wait_recv()
        send_first(link, s)
        if k:
            relay_and_put(order[k - 1])
    relay_and_put(order[-1])

    link2 = links(1)

    def square_slot(s, carry):
        def step(m, carry):
            here = pl.ds(pl.multiple_of(m * chunk, chunk), chunk)
            own2[s, here, :] = multiply(own, oth, s, m * chunk)
            return carry
        lax.fori_loop(0, rows // chunk, step, 0)
        send_first(link2, s)
        return carry

    lax.fori_loop(0, slots, square_slot, 0)

    for k in range(1, slots):
        z_copy(k).wait_send()
    for s in range(slots):
        wait_sends(link, s)

    a, b, q = mixing_ref[0], mixing_ref[1], mixing_ref[2]
    eye = (
        lax.broadcasted_iota(jnp.int32, (width, width), 0) == lax.broadcasted_iota(jnp.int32, (width, width), 1)
    ).astype(jnp.float32)

    def mix(dense, square, s, holds_diag):
        def step(g, carry):
            scale = jnp.where(jnp.logical_and(holds_diag, g == base0 + s), a, 0.0)
            dense[s, group(g), :] = (
                scale * eye
                + b * dense[s, group(g), :].astype(jnp.float32)
                + q * square[s, group(g), :].astype(jnp.float32)
            ).astype(jnp.bfloat16)
            return carry
        lax.fori_loop(0, half, step, 0)

    for s in range(slots):
        mix(own, own2, s, diag)
    for s in range(slots):
        link2["core"](s).wait_recv()
        mix(oth, oth2, s, jnp.logical_not(diag))

    staged = yn
    n_chunk = rows // chunk

    def back(s, m):
        here = pl.ds(pl.multiple_of(m * chunk, chunk), chunk)
        return remote(
            staged.at[s, here], out_ref.at[z, here], p_send.at[s, m], p_recv.at[z, m], {"inner": s}
        )

    def back_arrival(s, m):
        here = pl.ds(pl.multiple_of(m * chunk, chunk), chunk)
        return remote(
            staged.at[s, here], out_ref.at[s, here], p_send.at[s, m], p_recv.at[s, m], {"inner": s}
        )

    def back_here(m):
        here = pl.ds(pl.multiple_of(m * chunk, chunk), chunk)
        return pltpu.make_async_copy(staged.at[z, here], out_ref.at[z, here], out_sem.at[m])

    def filter_tile(base):
        first = base // (half // n_chunk)

        def step(i, carry):
            m = first + i // slots
            s = i % slots
            here = pl.ds(pl.multiple_of(m * chunk, chunk), chunk)
            staged[s, here, :] = multiply(own, oth, s, m * chunk)

            @pl.when(s == z)
            def _():
                back_here(m).start()

            @pl.when(s != z)
            def _():
                back(s, m).start()
            return carry
        lax.fori_loop(0, (n_chunk // 2) * slots, step, 0)

    @pl.when(diag)
    def _():
        for s in range(slots):
            put_same(own2, s)
            put_flipped(oth2, s, base0)
        filter_tile(base0)
        for s in range(slots):
            relay_dt(link2, s)
            put_dt(dt2, s)
        for s in range(slots):
            link2["xo_relay"](s).wait_recv()
            put_flipped(xo2, s, base1)
        filter_tile(base1)

    @pl.when(jnp.logical_not(diag))
    def _():
        for s in range(slots):
            put_plain(own2, s, base0)
        for s in range(slots):
            relay_xo(link2, s)
            put_plain(xo2, s, base1)
        for s in range(slots):
            link2["yn"](s).wait_recv()
            put_same(yn2, s)
        filter_tile(base0)
        for s in range(slots):
            link2["dt_y"](s).wait_recv()
            put_dt(dt2, s)
        filter_tile(base1)

    for s in range(slots):
        wait_sends(link2, s)
    for m in range(n_chunk):
        back_here(m).wait()
        for k in range(1, slots):
            back(others(k), m).wait_send()
        for k in range(1, slots):
            back_arrival(others(k), m).wait_recv()


def plane_filter(density, block_cols, mixing, row_start):
    row_count = density.shape[0]
    width = density.shape[2]
    slots = GS
    half = row_count // GS
    first_group = row_start // GS
    leaders = lax.dynamic_slice_in_dim(block_cols[:GS], first_group, half, 1)
    ordered = density[:, 0][(leaders - row_start).reshape(-1)]
    ordered = ordered.reshape(GS, half * width, width)
    rows = half * width
    panel = pltpu.VMEM((slots, rows, width), jnp.bfloat16)
    part = pltpu.VMEM((slots, rows // 2, width), jnp.bfloat16)
    dma = pltpu.SemaphoreType.DMA
    returned = pl.pallas_call(
        functools.partial(product_kernel, slots, half, width),
        out_shape=jax.ShapeDtypeStruct((slots, rows, width), jnp.bfloat16),
        in_specs=[pl.BlockSpec(memory_space=pltpu.SMEM), pl.BlockSpec(memory_space=pl.ANY)],
        out_specs=pl.BlockSpec(memory_space=pl.ANY),
        scratch_shapes=[
            pltpu.VMEM((2 * half, rows, width), jnp.bfloat16),
            panel, panel, panel, panel, part,
            panel, panel, panel, panel, part,
            dma((slots,)), dma((slots,)), dma, dma((2, 4, slots)), dma((2, 4, slots)),
            dma((slots, 4)), dma((slots, 4)), dma((4,)),
        ],
        compiler_params=pltpu.CompilerParams(
            collective_id=0, has_side_effects=True, vmem_limit_bytes=60 * 1024 * 1024
        ),
        cost_estimate=pl.CostEstimate(
            flops=8 * rows * rows * 2 * slots * width, bytes_accessed=4 * slots * rows * width, transcendentals=0
        ),
    )(mixing, ordered)
    regrouped = returned.reshape(GS * half, 1, width, width)
    local_rows = row_start + jnp.arange(row_count, dtype=jnp.int32)
    clique_ids = lax.dynamic_slice_in_dim(block_cols[:, 0], row_start, row_count, 0)
    positions = clique_ids * half + (local_rows // GS - first_group)
    return regrouped[positions]


def body(form, density, block_cols, mixing):
    row_count = density.shape[0]
    row_start = lax.axis_index("row") * row_count
    return form(density, block_cols, mixing, row_start)


def solution(mesh):
    in_specs = (P("row", ("col", "inner"), None, None), P(), P())
    out_specs = P("row", ("col", "inner"), None, None)
    by_plane = mesh.shape["row"] == 2 and mesh.shape["col"] == 4 and mesh.shape["inner"] == GS
    form = plane_filter if by_plane else clique_filter
    return jax.shard_map(
        functools.partial(body, form), mesh=mesh, in_specs=in_specs, out_specs=out_specs, check_vma=False
    )
```

```python
import functools

import jax
import jax.numpy as jnp
from jax import lax
from jax.experimental import pallas as pl
from jax.experimental.pallas import tpu as pltpu
from jax.sharding import PartitionSpec as P

GS = 4


def fold_with(panel, piece):
    return jnp.einsum("htab,tgbc->hgac", panel, piece, preferred_element_type=jnp.float32)


def clique_filter(density, block_cols, mixing, row_start):
    row_count = density.shape[0]
    width = density.shape[2]
    groups_here = row_count // GS
    first_group = row_start // GS
    leaders = lax.dynamic_slice_in_dim(block_cols[:GS], first_group, groups_here, 1)
    ordered = density[:, 0][(leaders - row_start).reshape(-1)]
    ordered = ordered.reshape(GS, groups_here, 1, width, width)
    arrived = lax.all_to_all(ordered, "inner", split_axis=0, concat_axis=2, tiled=True)
    blocks = arrived[0]
    slot_count = blocks.shape[1]
    slot_start = lax.axis_index("col") * slot_count
    density_panel = lax.all_gather(blocks, "col", axis=1, tiled=True)
    square = fold_with(density_panel, lax.all_gather(blocks, "row", axis=0, tiled=True)).astype(
        jnp.bfloat16
    )
    group_ids = first_group + jnp.arange(groups_here, dtype=jnp.int32)
    slot_ids = slot_start + jnp.arange(slot_count, dtype=jnp.int32)
    on_diagonal = (group_ids[:, None] == slot_ids[None, :]).astype(jnp.float32)
    identity = jnp.eye(width, dtype=jnp.float32)
    mixer_blocks = (
        mixing[0] * on_diagonal[:, :, None, None] * identity
        + mixing[1] * blocks.astype(jnp.float32)
        + mixing[2] * square.astype(jnp.float32)
    ).astype(jnp.bfloat16)
    square_panel = lax.all_gather(square, "col", axis=1, tiled=True)
    filtered = fold_with(
        square_panel, lax.all_gather(mixer_blocks, "row", axis=0, tiled=True)
    ).astype(jnp.bfloat16)
    returned = lax.all_to_all(filtered[None], "inner", split_axis=2, concat_axis=0, tiled=True)
    regrouped = returned.reshape(GS * groups_here, 1, width, width)
    local_rows = row_start + jnp.arange(row_count, dtype=jnp.int32)
    clique_ids = lax.dynamic_slice_in_dim(block_cols[:, 0], row_start, row_count, 0)
    positions = clique_ids * groups_here + (local_rows // GS - first_group)
    return regrouped[positions]


def product_kernel(
    slots, half, width, mixing_ref, ordered_ref, out_ref,
    left, panel, xo, yn, dt, own2, oth2, xo2, yn2, dt2,
    z_send, z_recv, in_sem, send_sems, recv_sems, p_send, p_recv, out_sem,
):
    tile = half // 2
    rows = half * width
    r = lax.axis_index("row")
    c = lax.axis_index("col")
    z = lax.axis_index("inner")
    y, x = c // 2, c % 2
    to_x = {"col": y * 2 + (1 - x)}
    to_y = {"col": (1 - y) * 2 + x}
    to_core = {"row": 1 - r}
    base0 = x * tile
    base1 = (1 - x) * tile
    diag = r == y
    MESH = pl.DeviceIdType.MESH

    def others(k):
        return (z + k) % slots

    own = panel.at[:, pl.ds(0, rows)]
    oth = panel.at[:, pl.ds(rows, rows)]

    barrier = pltpu.get_barrier_semaphore()
    for k in range(1, slots):
        pl.semaphore_signal(barrier, inc=1, device_id={"inner": others(k)}, device_id_type=MESH)
    for target in (to_x, to_y, to_core):
        pl.semaphore_signal(barrier, inc=1, device_id=target, device_id_type=MESH)
    pl.semaphore_wait(barrier, slots - 1 + 3)

    def remote(src, dst, send, recv, target):
        return pltpu.make_async_remote_copy(
            src_ref=src, dst_ref=dst, send_sem=send, recv_sem=recv, device_id=target, device_id_type=MESH
        )

    def z_copy(k):
        to = others(k)
        return remote(ordered_ref.at[to], own.at[z], z_send.at[k], z_recv.at[z], {"inner": to})

    def z_arrival(s):
        return remote(ordered_ref.at[s], own.at[s], z_send.at[0], z_recv.at[s], {"inner": s})

    for k in range(1, slots):
        z_copy(k).start()
    keep = pltpu.make_async_copy(ordered_ref.at[z], own.at[z], in_sem)
    keep.start()

    def links(phase):
        mine, oth_, xo_, yn_, dt_ = ((own, oth, xo, yn, dt), (own2, oth2, xo2, yn2, dt2))[phase]
        diag_rows = pl.ds(pl.multiple_of(base0 * width, width), tile * width)

        def make(kind, index, src, dst, target):
            return lambda s: remote(
                src(s), dst.at[s], send_sems.at[phase, index, s], recv_sems.at[phase, kind, s], target
            )

        return dict(
            core=make(0, 0, lambda s: mine.at[s], oth_, to_core),
            xo=make(1, 1, lambda s: mine.at[s], xo_, to_x),
            yn=make(2, 2, lambda s: mine.at[s], yn_, to_y),
            dt=make(3, 3, lambda s: mine.at[s, diag_rows], dt_, to_x),
            dt_y=make(3, 1, lambda s: dt_.at[s], dt_, to_y),
            xo_relay=make(1, 2, lambda s: xo_.at[s], xo_, to_core),
        )

    def send_first(link, s):
        @pl.when(diag)
        def _():
            link["yn"](s).start()
            link["dt"](s).start()
            link["core"](s).start()

        @pl.when(jnp.logical_not(diag))
        def _():
            link["xo"](s).start()
            link["core"](s).start()

    def wait_sends(link, s):
        @pl.when(diag)
        def _():
            for name in ("yn", "dt", "core", "dt_y"):
                link[name](s).wait_send()

        @pl.when(jnp.logical_not(diag))
        def _():
            for name in ("xo", "core", "xo_relay"):
                link[name](s).wait_send()

    def relay_dt(link, s):
        link["dt"](s).wait_recv()
        link["dt_y"](s).start()

    def relay_xo(link, s):
        link["xo"](s).wait_recv()
        link["xo_relay"](s).start()

    def group(g):
        return pl.ds(pl.multiple_of(g * width, width), width)

    def put_same(source, s):
        def step(g, carry):
            left[group(g), group(base0 + s)] = source[s, group(g), :]
            return carry
        lax.fori_loop(0, half, step, 0)

        def flip(g, carry):
            left[group(base0 + s), group(base1 + g)] = source[s, group(base1 + g), :].T
            return carry
        lax.fori_loop(0, tile, flip, 0)

    def put_dt(source, s):
        def step(g, carry):
            left[group(base1 + g), group(base1 + s)] = source[s, group(g), :]
            return carry
        lax.fori_loop(0, tile, step, 0)

    def put_flipped(source, s, base):
        def step(g, carry):
            left[group(base + s), group(half + g)] = source[s, group(g), :].T
            return carry
        lax.fori_loop(0, half, step, 0)

    def put_plain(source, s, base):
        def step(g, carry):
            left[group(g), group(half + base + s)] = source[s, group(g), :]
            return carry
        lax.fori_loop(0, half, step, 0)

    chunk = rows // 4

    def multiply(s, row_start):
        here = pl.ds(pl.multiple_of(row_start, chunk), chunk)
        return jnp.dot(left[here, :], panel[s], preferred_element_type=jnp.float32).astype(jnp.bfloat16)

    link = links(0)
    order = [z, z + 1 - 2 * (z % 2), (z + 2) % 4, 3 - z] if slots == 4 else [others(k) for k in range(slots)]

    def relay_and_put(s):
        @pl.when(diag)
        def _():
            relay_dt(link, s)
            put_same(own, s)
            put_dt(dt, s)
            link["core"](s).wait_recv()
            put_flipped(oth, s, base0)
            link["xo_relay"](s).wait_recv()
            put_flipped(xo, s, base1)

        @pl.when(jnp.logical_not(diag))
        def _():
            relay_xo(link, s)
            put_plain(own, s, base0)
            put_plain(xo, s, base1)
            link["yn"](s).wait_recv()
            put_same(yn, s)
            link["dt_y"](s).wait_recv()
            put_dt(dt, s)
            link["core"](s).wait_recv()

    for k, s in enumerate(order):
        if k == 0:
            keep.wait()
        else:
            z_arrival(s).wait_recv()
        send_first(link, s)
        if k:
            relay_and_put(order[k - 1])
    relay_and_put(order[-1])

    link2 = links(1)
    for s in range(slots):
        wait_sends(link, s)
    a, b, q = mixing_ref[0], mixing_ref[1], mixing_ref[2]
    eye = (
        lax.broadcasted_iota(jnp.int32, (width, width), 0) == lax.broadcasted_iota(jnp.int32, (width, width), 1)
    ).astype(jnp.float32)

    def combine(dense, square):
        return b * dense.astype(jnp.float32) + q * square.astype(jnp.float32)

    def mix(dense, square, s, holds_diag):
        def step(g, carry):
            scale = jnp.where(jnp.logical_and(holds_diag, g == base0 + s), a, 0.0)
            dense[s, group(g), :] = (
                scale * eye + combine(dense[s, group(g), :], square[s, group(g), :])
            ).astype(jnp.bfloat16)
            return carry
        lax.fori_loop(0, half, step, 0)

    def square_slot(s, carry):
        def step(m, carry):
            here = pl.ds(pl.multiple_of(m * chunk, chunk), chunk)
            own2[s, here, :] = multiply(s, m * chunk)
            return carry
        lax.fori_loop(0, rows // chunk, step, 0)
        send_first(link2, s)
        mix(own, own2, s, diag)
        return carry

    lax.fori_loop(0, slots, square_slot, 0)

    for k in range(1, slots):
        z_copy(k).wait_send()
    for s in range(slots):
        link2["core"](s).wait_recv()
        mix(oth, oth2, s, jnp.logical_not(diag))

    staged = yn
    n_chunk = rows // chunk

    def back(s, m):
        here = pl.ds(pl.multiple_of(m * chunk, chunk), chunk)
        return remote(
            staged.at[s, here], out_ref.at[z, here], p_send.at[s, m], p_recv.at[z, m], {"inner": s}
        )

    def back_arrival(s, m):
        here = pl.ds(pl.multiple_of(m * chunk, chunk), chunk)
        return remote(
            staged.at[s, here], out_ref.at[s, here], p_send.at[s, m], p_recv.at[s, m], {"inner": s}
        )

    def back_here(m):
        here = pl.ds(pl.multiple_of(m * chunk, chunk), chunk)
        return pltpu.make_async_copy(staged.at[z, here], out_ref.at[z, here], out_sem.at[m])

    def filter_tile(base):
        first = base // (half // n_chunk)

        def step(i, carry):
            m = first + i // slots
            s = i % slots
            here = pl.ds(pl.multiple_of(m * chunk, chunk), chunk)
            staged[s, here, :] = multiply(s, m * chunk)

            @pl.when(s == z)
            def _():
                back_here(m).start()

            @pl.when(s != z)
            def _():
                back(s, m).start()
            return carry
        lax.fori_loop(0, (n_chunk // 2) * slots, step, 0)

    @pl.when(diag)
    def _():
        for s in range(slots):
            put_same(own2, s)
            put_flipped(oth2, s, base0)
        filter_tile(base0)
        for s in range(slots):
            relay_dt(link2, s)
            put_dt(dt2, s)
        for s in range(slots):
            link2["xo_relay"](s).wait_recv()
            put_flipped(xo2, s, base1)
        filter_tile(base1)

    @pl.when(jnp.logical_not(diag))
    def _():
        for s in range(slots):
            put_plain(own2, s, base0)
        for s in range(slots):
            relay_xo(link2, s)
            put_plain(xo2, s, base1)
        for s in range(slots):
            link2["yn"](s).wait_recv()
            put_same(yn2, s)
        filter_tile(base0)
        for s in range(slots):
            link2["dt_y"](s).wait_recv()
            put_dt(dt2, s)
        filter_tile(base1)

    for s in range(slots):
        wait_sends(link2, s)
    for m in range(n_chunk):
        back_here(m).wait()
        for k in range(1, slots):
            back(others(k), m).wait_send()
        for k in range(1, slots):
            back_arrival(others(k), m).wait_recv()


def plane_filter(density, block_cols, mixing, row_start):
    row_count = density.shape[0]
    width = density.shape[2]
    slots = GS
    half = row_count // GS
    first_group = row_start // GS
    leaders = lax.dynamic_slice_in_dim(block_cols[:GS], first_group, half, 1)
    ordered = density[:, 0][(leaders - row_start).reshape(-1)]
    ordered = ordered.reshape(GS, half * width, width)
    rows = half * width
    panel = pltpu.VMEM((slots, rows, width), jnp.bfloat16)
    part = pltpu.VMEM((slots, rows // 2, width), jnp.bfloat16)
    dma = pltpu.SemaphoreType.DMA
    returned = pl.pallas_call(
        functools.partial(product_kernel, slots, half, width),
        out_shape=jax.ShapeDtypeStruct((slots, rows, width), jnp.bfloat16),
        in_specs=[pl.BlockSpec(memory_space=pltpu.SMEM), pl.BlockSpec(memory_space=pl.ANY)],
        out_specs=pl.BlockSpec(memory_space=pl.ANY),
        scratch_shapes=[
            pltpu.VMEM((rows, 2 * rows), jnp.bfloat16),
            pltpu.VMEM((slots, 2 * rows, width), jnp.bfloat16),
            panel, panel, part,
            panel, panel, panel, panel, part,
            dma((slots,)), dma((slots,)), dma, dma((2, 4, slots)), dma((2, 4, slots)),
            dma((slots, 4)), dma((slots, 4)), dma((4,)),
        ],
        compiler_params=pltpu.CompilerParams(
            collective_id=0, has_side_effects=True, vmem_limit_bytes=60 * 1024 * 1024
        ),
        cost_estimate=pl.CostEstimate(
            flops=8 * rows * rows * 2 * slots * width, bytes_accessed=4 * slots * rows * width, transcendentals=0
        ),
    )(mixing, ordered)
    regrouped = returned.reshape(GS * half, 1, width, width)
    local_rows = row_start + jnp.arange(row_count, dtype=jnp.int32)
    clique_ids = lax.dynamic_slice_in_dim(block_cols[:, 0], row_start, row_count, 0)
    positions = clique_ids * half + (local_rows // GS - first_group)
    return regrouped[positions]


def body(form, density, block_cols, mixing):
    row_count = density.shape[0]
    row_start = lax.axis_index("row") * row_count
    return form(density, block_cols, mixing, row_start)


def solution(mesh):
    in_specs = (P("row", ("col", "inner"), None, None), P(), P())
    out_specs = P("row", ("col", "inner"), None, None)
    by_plane = mesh.shape["row"] == 2 and mesh.shape["col"] == 4 and mesh.shape["inner"] == GS
    form = plane_filter if by_plane else clique_filter
    return jax.shard_map(
        functools.partial(body, form), mesh=mesh, in_specs=in_specs, out_specs=out_specs, check_vma=False
    )
```

```python
import functools

import jax
import jax.numpy as jnp
from jax import lax
from jax.experimental import pallas as pl
from jax.experimental.pallas import tpu as pltpu
from jax.sharding import PartitionSpec as P

GS = 4


def fold_with(panel, piece):
    return jnp.einsum("htab,tgbc->hgac", panel, piece, preferred_element_type=jnp.float32)


def clique_filter(density, block_cols, mixing, row_start):
    row_count = density.shape[0]
    width = density.shape[2]
    groups_here = row_count // GS
    first_group = row_start // GS
    leaders = lax.dynamic_slice_in_dim(block_cols[:GS], first_group, groups_here, 1)
    ordered = density[:, 0][(leaders - row_start).reshape(-1)]
    ordered = ordered.reshape(GS, groups_here, 1, width, width)
    arrived = lax.all_to_all(ordered, "inner", split_axis=0, concat_axis=2, tiled=True)
    blocks = arrived[0]
    slot_count = blocks.shape[1]
    slot_start = lax.axis_index("col") * slot_count
    density_panel = lax.all_gather(blocks, "col", axis=1, tiled=True)
    square = fold_with(density_panel, lax.all_gather(blocks, "row", axis=0, tiled=True)).astype(
        jnp.bfloat16
    )
    group_ids = first_group + jnp.arange(groups_here, dtype=jnp.int32)
    slot_ids = slot_start + jnp.arange(slot_count, dtype=jnp.int32)
    on_diagonal = (group_ids[:, None] == slot_ids[None, :]).astype(jnp.float32)
    identity = jnp.eye(width, dtype=jnp.float32)
    mixer_blocks = (
        mixing[0] * on_diagonal[:, :, None, None] * identity
        + mixing[1] * blocks.astype(jnp.float32)
        + mixing[2] * square.astype(jnp.float32)
    ).astype(jnp.bfloat16)
    square_panel = lax.all_gather(square, "col", axis=1, tiled=True)
    filtered = fold_with(
        square_panel, lax.all_gather(mixer_blocks, "row", axis=0, tiled=True)
    ).astype(jnp.bfloat16)
    returned = lax.all_to_all(filtered[None], "inner", split_axis=2, concat_axis=0, tiled=True)
    regrouped = returned.reshape(GS * groups_here, 1, width, width)
    local_rows = row_start + jnp.arange(row_count, dtype=jnp.int32)
    clique_ids = lax.dynamic_slice_in_dim(block_cols[:, 0], row_start, row_count, 0)
    positions = clique_ids * groups_here + (local_rows // GS - first_group)
    return regrouped[positions]


class Part:
    def __init__(self, ref, rows):
        self.ref, self.rows = ref, rows

    def __getitem__(self, slot):
        return self.ref.at[slot, self.rows]


def product_kernel(
    slots, half, width, mixing_ref, ordered_ref, out_ref,
    left, panel, xo, yn, dt, own2, oth2, xo2, yn2, dt2,
    z_send, z_recv, in_sem, send_sems, recv_sems, p_send, p_recv, out_sem,
):
    tile = half // 2
    rows = half * width
    r = lax.axis_index("row")
    c = lax.axis_index("col")
    z = lax.axis_index("inner")
    y, x = c // 2, c % 2
    to_x = {"col": y * 2 + (1 - x)}
    to_y = {"col": (1 - y) * 2 + x}
    to_core = {"row": 1 - r}
    base0 = x * tile
    base1 = (1 - x) * tile
    diag = r == y
    MESH = pl.DeviceIdType.MESH

    def others(k):
        return (z + k) % slots

    own = panel.at[:, pl.ds(0, rows)]
    oth = panel.at[:, pl.ds(rows, rows)]

    barrier = pltpu.get_barrier_semaphore()
    for k in range(1, slots):
        pl.semaphore_signal(barrier, inc=1, device_id={"inner": others(k)}, device_id_type=MESH)
    for target in (to_x, to_y, to_core):
        pl.semaphore_signal(barrier, inc=1, device_id=target, device_id_type=MESH)
    pl.semaphore_wait(barrier, slots - 1 + 3)

    def remote(src, dst, send, recv, target):
        return pltpu.make_async_remote_copy(
            src_ref=src, dst_ref=dst, send_sem=send, recv_sem=recv, device_id=target, device_id_type=MESH
        )

    order = [z, z + 1 - 2 * (z % 2), (z + slots // 2) % slots, slots - 1 - z]

    def z_copy(k):
        to = order[k]
        return remote(ordered_ref.at[to], own.at[z], z_send.at[k], z_recv.at[z], {"inner": to})

    def z_arrival(s):
        return remote(ordered_ref.at[s], own.at[s], z_send.at[0], z_recv.at[s], {"inner": s})

    z_copy(2).start()
    z_copy(1).start()
    keep = pltpu.make_async_copy(ordered_ref.at[z], own.at[z], in_sem)
    keep.start()

    def links(phase):
        mine, oth_, xo_, yn_, dt_ = ((own, oth, xo, yn, dt), (own2, oth2, xo2, yn2, dt2))[phase]
        rows0 = pl.ds(pl.multiple_of(base0 * width, width), tile * width)
        rows1 = pl.ds(pl.multiple_of(base1 * width, width), tile * width)

        def make(kind, index, src, dst, target):
            return lambda s: remote(
                src(s), dst[s], send_sems.at[phase, index, s], recv_sems.at[phase, kind, s], target
            )

        return dict(
            core=make(0, 0, lambda s: mine.at[s], oth_.at, to_core),
            xo0=make(1, 1, lambda s: mine.at[s, rows1], Part(xo_, rows1), to_x),
            xo1=make(4, 3, lambda s: mine.at[s, rows0], Part(xo_, rows0), to_x),
            yn=make(2, 2, lambda s: mine.at[s], yn_.at, to_y),
            dt=make(3, 3, lambda s: mine.at[s, rows0], dt_.at, to_x),
            dt_y=make(3, 1, lambda s: dt_.at[s], dt_.at, to_y),
            xo0_relay=make(1, 2, lambda s: xo_.at[s, rows0], Part(xo_, rows0), to_core),
            xo1_relay=make(4, 4, lambda s: xo_.at[s, rows1], Part(xo_, rows1), to_core),
        )

    def send_first(link, s):
        @pl.when(diag)
        def _():
            link["yn"](s).start()
            link["dt"](s).start()
            link["core"](s).start()

        @pl.when(jnp.logical_not(diag))
        def _():
            link["xo0"](s).start()
            link["core"](s).start()

    def wait_sends(link, s):
        @pl.when(diag)
        def _():
            for name in ("yn", "dt", "core", "dt_y"):
                link[name](s).wait_send()

        @pl.when(jnp.logical_not(diag))
        def _():
            for name in ("xo0", "xo1", "core", "xo0_relay", "xo1_relay"):
                link[name](s).wait_send()

    def relay_dt(link, s):
        link["dt"](s).wait_recv()
        link["dt_y"](s).start()

    def relay_xo(link, s, part):
        link[("xo0", "xo1")[part]](s).wait_recv()
        link[("xo0_relay", "xo1_relay")[part]](s).start()

    def send_second(link, s):
        @pl.when(jnp.logical_not(diag))
        def _():
            link["xo1"](s).start()

    def group(g):
        return pl.ds(pl.multiple_of(g * width, width), width)

    def put_same(source, s):
        def step(g, carry):
            left[group(g), group(base0 + s)] = source[s, group(g), :]
            return carry
        lax.fori_loop(0, half, step, 0)

        def flip(g, carry):
            left[group(base0 + s), group(base1 + g)] = source[s, group(base1 + g), :].T
            return carry
        lax.fori_loop(0, tile, flip, 0)

    def put_dt(source, s):
        def step(g, carry):
            left[group(base1 + g), group(base1 + s)] = source[s, group(g), :]
            return carry
        lax.fori_loop(0, tile, step, 0)

    def put_flipped(source, s, base):
        def step(g, carry):
            left[group(base + s), group(half + g)] = source[s, group(g), :].T
            return carry
        lax.fori_loop(0, half, step, 0)

    def put_plain(source, s, base, first, count):
        def step(g, carry):
            left[group(first + g), group(half + base + s)] = source[s, group(first + g), :]
            return carry
        lax.fori_loop(0, count, step, 0)

    chunk = rows // 4

    def multiply(s, row_start):
        here = pl.ds(pl.multiple_of(row_start, chunk), chunk)
        return jnp.dot(left[here, :], panel[s], preferred_element_type=jnp.float32).astype(jnp.bfloat16)

    link = links(0)

    def relay_and_put(s):
        @pl.when(diag)
        def _():
            relay_dt(link, s)
            put_same(own, s)
            put_dt(dt, s)
            link["core"](s).wait_recv()
            put_flipped(oth, s, base0)
            link["xo0_relay"](s).wait_recv()
            link["xo1_relay"](s).wait_recv()
            put_flipped(xo, s, base1)

        @pl.when(jnp.logical_not(diag))
        def _():
            relay_xo(link, s, 0)
            relay_xo(link, s, 1)
            put_plain(own, s, base0, 0, half)
            put_plain(xo, s, base1, 0, half)
            link["yn"](s).wait_recv()
            put_same(yn, s)
            link["dt_y"](s).wait_recv()
            put_dt(dt, s)
            link["core"](s).wait_recv()

    for k, s in enumerate(order):
        if k == 0:
            keep.wait()
        else:
            if k == 2:
                z_copy(2).wait_send()
                z_copy(3).start()
            z_arrival(s).wait_recv()
        send_first(link, s)
        send_second(link, s)
        if k:
            relay_and_put(order[k - 1])
    relay_and_put(order[-1])

    link2 = links(1)
    for s in range(slots):
        wait_sends(link, s)
    a, b, q = mixing_ref[0], mixing_ref[1], mixing_ref[2]
    eye = (
        lax.broadcasted_iota(jnp.int32, (width, width), 0) == lax.broadcasted_iota(jnp.int32, (width, width), 1)
    ).astype(jnp.float32)

    def combine(dense, square):
        return b * dense.astype(jnp.float32) + q * square.astype(jnp.float32)

    def mix(dense, square, s, holds_diag):
        def step(g, carry):
            scale = jnp.where(jnp.logical_and(holds_diag, g == base0 + s), a, 0.0)
            dense[s, group(g), :] = (
                scale * eye + combine(dense[s, group(g), :], square[s, group(g), :])
            ).astype(jnp.bfloat16)
            return carry
        lax.fori_loop(0, half, step, 0)

    def square_slot(s, carry):
        def step(m, carry):
            here = pl.ds(pl.multiple_of(m * chunk, chunk), chunk)
            own2[s, here, :] = multiply(s, m * chunk)
            return carry
        lax.fori_loop(0, rows // chunk, step, 0)
        send_first(link2, s)
        mix(own, own2, s, diag)
        return carry

    lax.fori_loop(0, slots, square_slot, 0)
    for s in range(slots):
        send_second(link2, s)

    for k in (1, 3):
        z_copy(k).wait_send()
    for s in range(slots):
        link2["core"](s).wait_recv()
        mix(oth, oth2, s, jnp.logical_not(diag))

    staged = yn
    n_chunk = rows // chunk

    def back(s, m):
        here = pl.ds(pl.multiple_of(m * chunk, chunk), chunk)
        return remote(
            staged.at[s, here], out_ref.at[z, here], p_send.at[s, m], p_recv.at[z, m], {"inner": s}
        )

    def back_arrival(s, m):
        here = pl.ds(pl.multiple_of(m * chunk, chunk), chunk)
        return remote(
            staged.at[s, here], out_ref.at[s, here], p_send.at[s, m], p_recv.at[s, m], {"inner": s}
        )

    def back_here(m):
        here = pl.ds(pl.multiple_of(m * chunk, chunk), chunk)
        return pltpu.make_async_copy(staged.at[z, here], out_ref.at[z, here], out_sem.at[m])

    def filter_tile(base):
        first = base // (half // n_chunk)

        def step(i, carry):
            m = first + i // slots
            s = i % slots
            here = pl.ds(pl.multiple_of(m * chunk, chunk), chunk)
            staged[s, here, :] = multiply(s, m * chunk)

            @pl.when(s == z)
            def _():
                back_here(m).start()

            @pl.when(s != z)
            def _():
                back(s, m).start()
            return carry
        lax.fori_loop(0, (n_chunk // 2) * slots, step, 0)

    @pl.when(diag)
    def _():
        for s in range(slots):
            put_same(own2, s)
            put_flipped(oth2, s, base0)
        filter_tile(base0)
        for s in range(slots):
            relay_dt(link2, s)
            put_dt(dt2, s)
        for s in range(slots):
            link2["xo0_relay"](s).wait_recv()
            link2["xo1_relay"](s).wait_recv()
            put_flipped(xo2, s, base1)
        filter_tile(base1)

    @pl.when(jnp.logical_not(diag))
    def _():
        for s in range(slots):
            put_plain(own2, s, base0, 0, half)
        for s in range(slots):
            relay_xo(link2, s, 0)
            put_plain(xo2, s, base1, base0, tile)
        for s in range(slots):
            link2["yn"](s).wait_recv()
            put_same(yn2, s)
        filter_tile(base0)
        for s in range(slots):
            relay_xo(link2, s, 1)
            put_plain(xo2, s, base1, base1, tile)
        for s in range(slots):
            link2["dt_y"](s).wait_recv()
            put_dt(dt2, s)
        filter_tile(base1)

    for s in range(slots):
        wait_sends(link2, s)
    for m in range(n_chunk):
        back_here(m).wait()
        for k in range(1, slots):
            back(others(k), m).wait_send()
        for k in range(1, slots):
            back_arrival(others(k), m).wait_recv()


def plane_filter(density, block_cols, mixing, row_start):
    row_count = density.shape[0]
    width = density.shape[2]
    slots = GS
    half = row_count // GS
    first_group = row_start // GS
    leaders = lax.dynamic_slice_in_dim(block_cols[:GS], first_group, half, 1)
    ordered = density[:, 0][(leaders - row_start).reshape(-1)]
    ordered = ordered.reshape(GS, half * width, width)
    rows = half * width
    panel = pltpu.VMEM((slots, rows, width), jnp.bfloat16)
    part = pltpu.VMEM((slots, rows // 2, width), jnp.bfloat16)
    dma = pltpu.SemaphoreType.DMA
    returned = pl.pallas_call(
        functools.partial(product_kernel, slots, half, width),
        out_shape=jax.ShapeDtypeStruct((slots, rows, width), jnp.bfloat16),
        in_specs=[pl.BlockSpec(memory_space=pltpu.SMEM), pl.BlockSpec(memory_space=pl.ANY)],
        out_specs=pl.BlockSpec(memory_space=pl.ANY),
        scratch_shapes=[
            pltpu.VMEM((rows, 2 * rows), jnp.bfloat16),
            pltpu.VMEM((slots, 2 * rows, width), jnp.bfloat16),
            panel, panel, part,
            panel, panel, panel, panel, part,
            dma((slots,)), dma((slots,)), dma, dma((2, 5, slots)), dma((2, 5, slots)),
            dma((slots, 4)), dma((slots, 4)), dma((4,)),
        ],
        compiler_params=pltpu.CompilerParams(
            collective_id=0, has_side_effects=True, vmem_limit_bytes=60 * 1024 * 1024
        ),
        cost_estimate=pl.CostEstimate(
            flops=8 * rows * rows * 2 * slots * width, bytes_accessed=4 * slots * rows * width, transcendentals=0
        ),
    )(mixing, ordered)
    regrouped = returned.reshape(GS * half, 1, width, width)
    local_rows = row_start + jnp.arange(row_count, dtype=jnp.int32)
    clique_ids = lax.dynamic_slice_in_dim(block_cols[:, 0], row_start, row_count, 0)
    positions = clique_ids * half + (local_rows // GS - first_group)
    return regrouped[positions]


def body(form, density, block_cols, mixing):
    row_count = density.shape[0]
    row_start = lax.axis_index("row") * row_count
    return form(density, block_cols, mixing, row_start)


def solution(mesh):
    in_specs = (P("row", ("col", "inner"), None, None), P(), P())
    out_specs = P("row", ("col", "inner"), None, None)
    by_plane = mesh.shape["row"] == 2 and mesh.shape["col"] == 4 and mesh.shape["inner"] == GS
    form = plane_filter if by_plane else clique_filter
    return jax.shard_map(
        functools.partial(body, form), mesh=mesh, in_specs=in_specs, out_specs=out_specs, check_vma=False
    )
```

```python
import functools

import jax
import jax.numpy as jnp
from jax import lax
from jax.experimental import pallas as pl
from jax.experimental.pallas import tpu as pltpu
from jax.sharding import PartitionSpec as P

GS = 4


def fold_with(panel, piece):
    return jnp.einsum("htab,tgbc->hgac", panel, piece, preferred_element_type=jnp.float32)


def clique_filter(density, block_cols, mixing, row_start):
    row_count = density.shape[0]
    width = density.shape[2]
    groups_here = row_count // GS
    first_group = row_start // GS
    leaders = lax.dynamic_slice_in_dim(block_cols[:GS], first_group, groups_here, 1)
    ordered = density[:, 0][(leaders - row_start).reshape(-1)]
    ordered = ordered.reshape(GS, groups_here, 1, width, width)
    arrived = lax.all_to_all(ordered, "inner", split_axis=0, concat_axis=2, tiled=True)
    blocks = arrived[0]
    slot_count = blocks.shape[1]
    slot_start = lax.axis_index("col") * slot_count
    density_panel = lax.all_gather(blocks, "col", axis=1, tiled=True)
    square = fold_with(density_panel, lax.all_gather(blocks, "row", axis=0, tiled=True)).astype(
        jnp.bfloat16
    )
    group_ids = first_group + jnp.arange(groups_here, dtype=jnp.int32)
    slot_ids = slot_start + jnp.arange(slot_count, dtype=jnp.int32)
    on_diagonal = (group_ids[:, None] == slot_ids[None, :]).astype(jnp.float32)
    identity = jnp.eye(width, dtype=jnp.float32)
    mixer_blocks = (
        mixing[0] * on_diagonal[:, :, None, None] * identity
        + mixing[1] * blocks.astype(jnp.float32)
        + mixing[2] * square.astype(jnp.float32)
    ).astype(jnp.bfloat16)
    square_panel = lax.all_gather(square, "col", axis=1, tiled=True)
    filtered = fold_with(
        square_panel, lax.all_gather(mixer_blocks, "row", axis=0, tiled=True)
    ).astype(jnp.bfloat16)
    returned = lax.all_to_all(filtered[None], "inner", split_axis=2, concat_axis=0, tiled=True)
    regrouped = returned.reshape(GS * groups_here, 1, width, width)
    local_rows = row_start + jnp.arange(row_count, dtype=jnp.int32)
    clique_ids = lax.dynamic_slice_in_dim(block_cols[:, 0], row_start, row_count, 0)
    positions = clique_ids * groups_here + (local_rows // GS - first_group)
    return regrouped[positions]


class Part:
    def __init__(self, ref, rows):
        self.ref, self.rows = ref, rows

    def __getitem__(self, slot):
        return self.ref.at[slot, self.rows]


def product_kernel(
    slots, half, width, mixing_ref, ordered_ref, out_ref,
    left, panel, xo, yn, dt, own2, oth2, xo2, yn2, dt2,
    z_send, z_recv, in_sem, send_sems, recv_sems, p_send, p_recv, out_sem,
):
    tile = half // 2
    rows = half * width
    r = lax.axis_index("row")
    c = lax.axis_index("col")
    z = lax.axis_index("inner")
    y, x = c // 2, c % 2
    to_x = {"col": y * 2 + (1 - x)}
    to_y = {"col": (1 - y) * 2 + x}
    to_core = {"row": 1 - r}
    base0 = x * tile
    base1 = (1 - x) * tile
    diag = r == y
    MESH = pl.DeviceIdType.MESH

    def others(k):
        return (z + k) % slots

    own = panel.at[:, pl.ds(0, rows)]
    oth = panel.at[:, pl.ds(rows, rows)]

    barrier = pltpu.get_barrier_semaphore()
    for k in range(1, slots):
        pl.semaphore_signal(barrier, inc=1, device_id={"inner": others(k)}, device_id_type=MESH)
    for target in (to_x, to_y, to_core):
        pl.semaphore_signal(barrier, inc=1, device_id=target, device_id_type=MESH)
    pl.semaphore_wait(barrier, slots - 1 + 3)

    def remote(src, dst, send, recv, target):
        return pltpu.make_async_remote_copy(
            src_ref=src, dst_ref=dst, send_sem=send, recv_sem=recv, device_id=target, device_id_type=MESH
        )

    def rank_of(v, k):
        return (v, v + 1 - 2 * (v % 2), (v + slots // 2) % slots, slots - 1 - v)[k]

    def group(g):
        return pl.ds(pl.multiple_of(g * width, width), width)

    order = [rank_of(z, k) for k in range(slots)]
    far_rows = pl.ds(pl.multiple_of(base1 * width, width), tile * width)

    def z_pieces(k, act):
        to = order[k]
        act(remote(
            ordered_ref.at[to, far_rows], own.at[z, far_rows], z_send.at[k, slots], z_recv.at[z, slots], {"inner": to}
        ))
        for j in range(slots):
            here = group(base0 + rank_of(to, j))
            copy = remote(
                ordered_ref.at[to, here], own.at[z, here], z_send.at[k, j], z_recv.at[z, j], {"inner": to}
            )
            if j >= k:
                act(copy)
            else:
                pl.when(jnp.logical_not(diag))(functools.partial(act, copy))

    def z_arrival(k):
        s = order[k]
        remote(
            ordered_ref.at[s, far_rows], own.at[s, far_rows], z_send.at[k, slots], z_recv.at[s, slots], {"inner": s}
        ).wait_recv()
        for j in range(slots):
            here = group(base0 + order[j])
            copy = remote(ordered_ref.at[s, here], own.at[s, here], z_send.at[k, j], z_recv.at[s, j], {"inner": s})
            if j >= k:
                copy.wait_recv()
            else:
                pl.when(jnp.logical_not(diag))(copy.wait_recv)

        @pl.when(diag)
        def _():
            for j in range(k):
                panel[s, group(base0 + order[j]), :] = panel[order[j], group(base0 + s), :].T

    def z_start(k):
        z_pieces(k, lambda copy: copy.start())

    def z_wait_send(k):
        z_pieces(k, lambda copy: copy.wait_send())

    z_start(2)
    z_start(1)
    keep = pltpu.make_async_copy(ordered_ref.at[z], own.at[z], in_sem)
    keep.start()

    def links(phase):
        mine, oth_, xo_, yn_, dt_ = ((own, oth, xo, yn, dt), (own2, oth2, xo2, yn2, dt2))[phase]
        rows0 = pl.ds(pl.multiple_of(base0 * width, width), tile * width)
        rows1 = pl.ds(pl.multiple_of(base1 * width, width), tile * width)

        def make(kind, index, src, dst, target):
            return lambda s: remote(
                src(s), dst[s], send_sems.at[phase, index, s], recv_sems.at[phase, kind, s], target
            )

        return dict(
            core=make(0, 0, lambda s: mine.at[s], oth_.at, to_core),
            xo0=make(1, 1, lambda s: mine.at[s, rows1], Part(xo_, rows1), to_x),
            xo1=make(4, 3, lambda s: mine.at[s, rows0], Part(xo_, rows0), to_x),
            yn=make(2, 2, lambda s: mine.at[s], yn_.at, to_y),
            dt=make(3, 3, lambda s: mine.at[s, rows0], dt_.at, to_x),
            dt_y=make(3, 1, lambda s: dt_.at[s], dt_.at, to_y),
            xo0_relay=make(1, 2, lambda s: xo_.at[s, rows0], Part(xo_, rows0), to_core),
            xo1_relay=make(4, 4, lambda s: xo_.at[s, rows1], Part(xo_, rows1), to_core),
        )

    def send_first(link, s):
        @pl.when(diag)
        def _():
            link["yn"](s).start()
            link["dt"](s).start()
            link["core"](s).start()

        @pl.when(jnp.logical_not(diag))
        def _():
            link["xo0"](s).start()
            link["core"](s).start()

    def wait_sends(link, s):
        @pl.when(diag)
        def _():
            for name in ("yn", "dt", "core", "dt_y"):
                link[name](s).wait_send()

        @pl.when(jnp.logical_not(diag))
        def _():
            for name in ("xo0", "xo1", "core", "xo0_relay", "xo1_relay"):
                link[name](s).wait_send()

    def relay_dt(link, s):
        link["dt"](s).wait_recv()
        link["dt_y"](s).start()

    def relay_xo(link, s, part):
        link[("xo0", "xo1")[part]](s).wait_recv()
        link[("xo0_relay", "xo1_relay")[part]](s).start()

    def send_second(link, s):
        @pl.when(jnp.logical_not(diag))
        def _():
            link["xo1"](s).start()

    def put_same(source, s):
        def step(g, carry):
            left[group(g), group(base0 + s)] = source[s, group(g), :]
            return carry
        lax.fori_loop(0, half, step, 0)

        def flip(g, carry):
            left[group(base0 + s), group(base1 + g)] = source[s, group(base1 + g), :].T
            return carry
        lax.fori_loop(0, tile, flip, 0)

    def put_dt(source, s):
        def step(g, carry):
            left[group(base1 + g), group(base1 + s)] = source[s, group(g), :]
            return carry
        lax.fori_loop(0, tile, step, 0)

    def put_flipped(source, s, base):
        def step(g, carry):
            left[group(base + s), group(half + g)] = source[s, group(g), :].T
            return carry
        lax.fori_loop(0, half, step, 0)

    def put_plain(source, s, base, first, count):
        def step(g, carry):
            left[group(first + g), group(half + base + s)] = source[s, group(first + g), :]
            return carry
        lax.fori_loop(0, count, step, 0)

    chunk = rows // 4

    def multiply(s, row_start):
        here = pl.ds(pl.multiple_of(row_start, chunk), chunk)
        return jnp.dot(left[here, :], panel[s], preferred_element_type=jnp.float32).astype(jnp.bfloat16)

    link = links(0)

    def relay_and_put(s):
        @pl.when(diag)
        def _():
            relay_dt(link, s)
            put_same(own, s)
            put_dt(dt, s)
            link["core"](s).wait_recv()
            put_flipped(oth, s, base0)
            link["xo0_relay"](s).wait_recv()
            link["xo1_relay"](s).wait_recv()
            put_flipped(xo, s, base1)

        @pl.when(jnp.logical_not(diag))
        def _():
            relay_xo(link, s, 0)
            relay_xo(link, s, 1)
            put_plain(own, s, base0, 0, half)
            put_plain(xo, s, base1, 0, half)
            link["yn"](s).wait_recv()
            put_same(yn, s)
            link["dt_y"](s).wait_recv()
            put_dt(dt, s)
            link["core"](s).wait_recv()

    for k, s in enumerate(order):
        if k == 0:
            keep.wait()
        else:
            if k == 2:
                z_wait_send(2)
                z_start(3)
            z_arrival(k)
        send_first(link, s)
        send_second(link, s)
        if k:
            relay_and_put(order[k - 1])
    relay_and_put(order[-1])

    link2 = links(1)
    for s in range(slots):
        wait_sends(link, s)
    a, b, q = mixing_ref[0], mixing_ref[1], mixing_ref[2]
    eye = (
        lax.broadcasted_iota(jnp.int32, (width, width), 0) == lax.broadcasted_iota(jnp.int32, (width, width), 1)
    ).astype(jnp.float32)

    def combine(dense, square):
        return b * dense.astype(jnp.float32) + q * square.astype(jnp.float32)

    def mix(dense, square, s, holds_diag):
        def step(g, carry):
            scale = jnp.where(jnp.logical_and(holds_diag, g == base0 + s), a, 0.0)
            dense[s, group(g), :] = (
                scale * eye + combine(dense[s, group(g), :], square[s, group(g), :])
            ).astype(jnp.bfloat16)
            return carry
        lax.fori_loop(0, half, step, 0)

    def square_slot(s, carry):
        def step(m, carry):
            here = pl.ds(pl.multiple_of(m * chunk, chunk), chunk)
            own2[s, here, :] = multiply(s, m * chunk)
            return carry
        lax.fori_loop(0, rows // chunk, step, 0)
        send_first(link2, s)
        mix(own, own2, s, diag)
        return carry

    lax.fori_loop(0, slots, square_slot, 0)
    for s in range(slots):
        send_second(link2, s)

    for k in (1, 3):
        z_wait_send(k)
    for s in range(slots):
        link2["core"](s).wait_recv()
        mix(oth, oth2, s, jnp.logical_not(diag))

    staged = yn
    n_chunk = rows // chunk

    def back(s, m):
        here = pl.ds(pl.multiple_of(m * chunk, chunk), chunk)
        return remote(
            staged.at[s, here], out_ref.at[z, here], p_send.at[s, m], p_recv.at[z, m], {"inner": s}
        )

    def back_arrival(s, m):
        here = pl.ds(pl.multiple_of(m * chunk, chunk), chunk)
        return remote(
            staged.at[s, here], out_ref.at[s, here], p_send.at[s, m], p_recv.at[s, m], {"inner": s}
        )

    def back_here(m):
        here = pl.ds(pl.multiple_of(m * chunk, chunk), chunk)
        return pltpu.make_async_copy(staged.at[z, here], out_ref.at[z, here], out_sem.at[m])

    def filter_tile(base):
        first = base // (half // n_chunk)

        def step(i, carry):
            m = first + i // slots
            s = i % slots
            here = pl.ds(pl.multiple_of(m * chunk, chunk), chunk)
            staged[s, here, :] = multiply(s, m * chunk)

            @pl.when(s == z)
            def _():
                back_here(m).start()

            @pl.when(s != z)
            def _():
                back(s, m).start()
            return carry
        lax.fori_loop(0, (n_chunk // 2) * slots, step, 0)

    @pl.when(diag)
    def _():
        for s in range(slots):
            put_same(own2, s)
            put_flipped(oth2, s, base0)
        filter_tile(base0)
        for s in range(slots):
            relay_dt(link2, s)
            put_dt(dt2, s)
        for s in range(slots):
            link2["xo0_relay"](s).wait_recv()
            link2["xo1_relay"](s).wait_recv()
            put_flipped(xo2, s, base1)
        filter_tile(base1)

    @pl.when(jnp.logical_not(diag))
    def _():
        for s in range(slots):
            put_plain(own2, s, base0, 0, half)
        for s in range(slots):
            relay_xo(link2, s, 0)
            put_plain(xo2, s, base1, base0, tile)
        for s in range(slots):
            link2["yn"](s).wait_recv()
            put_same(yn2, s)
        filter_tile(base0)
        for s in range(slots):
            relay_xo(link2, s, 1)
            put_plain(xo2, s, base1, base1, tile)
        for s in range(slots):
            link2["dt_y"](s).wait_recv()
            put_dt(dt2, s)
        filter_tile(base1)

    for s in range(slots):
        wait_sends(link2, s)
    for m in range(n_chunk):
        back_here(m).wait()
        for k in range(1, slots):
            back(others(k), m).wait_send()
        for k in range(1, slots):
            back_arrival(others(k), m).wait_recv()


def plane_filter(density, block_cols, mixing, row_start):
    row_count = density.shape[0]
    width = density.shape[2]
    slots = GS
    half = row_count // GS
    first_group = row_start // GS
    leaders = lax.dynamic_slice_in_dim(block_cols[:GS], first_group, half, 1)
    ordered = density[:, 0][(leaders - row_start).reshape(-1)]
    ordered = ordered.reshape(GS, half * width, width)
    rows = half * width
    panel = pltpu.VMEM((slots, rows, width), jnp.bfloat16)
    part = pltpu.VMEM((slots, rows // 2, width), jnp.bfloat16)
    dma = pltpu.SemaphoreType.DMA
    returned = pl.pallas_call(
        functools.partial(product_kernel, slots, half, width),
        out_shape=jax.ShapeDtypeStruct((slots, rows, width), jnp.bfloat16),
        in_specs=[pl.BlockSpec(memory_space=pltpu.SMEM), pl.BlockSpec(memory_space=pl.ANY)],
        out_specs=pl.BlockSpec(memory_space=pl.ANY),
        scratch_shapes=[
            pltpu.VMEM((rows, 2 * rows), jnp.bfloat16),
            pltpu.VMEM((slots, 2 * rows, width), jnp.bfloat16),
            panel, panel, part,
            panel, panel, panel, panel, part,
            dma((slots, slots + 1)), dma((slots, slots + 1)), dma, dma((2, 5, slots)), dma((2, 5, slots)),
            dma((slots, 4)), dma((slots, 4)), dma((4,)),
        ],
        compiler_params=pltpu.CompilerParams(
            collective_id=0, has_side_effects=True, vmem_limit_bytes=60 * 1024 * 1024
        ),
        cost_estimate=pl.CostEstimate(
            flops=8 * rows * rows * 2 * slots * width, bytes_accessed=4 * slots * rows * width, transcendentals=0
        ),
    )(mixing, ordered)
    regrouped = returned.reshape(GS * half, 1, width, width)
    local_rows = row_start + jnp.arange(row_count, dtype=jnp.int32)
    clique_ids = lax.dynamic_slice_in_dim(block_cols[:, 0], row_start, row_count, 0)
    positions = clique_ids * half + (local_rows // GS - first_group)
    return regrouped[positions]


def body(form, density, block_cols, mixing):
    row_count = density.shape[0]
    row_start = lax.axis_index("row") * row_count
    return form(density, block_cols, mixing, row_start)


def solution(mesh):
    in_specs = (P("row", ("col", "inner"), None, None), P(), P())
    out_specs = P("row", ("col", "inner"), None, None)
    by_plane = mesh.shape["row"] == 2 and mesh.shape["col"] == 4 and mesh.shape["inner"] == GS
    form = plane_filter if by_plane else clique_filter
    return jax.shard_map(
        functools.partial(body, form), mesh=mesh, in_specs=in_specs, out_specs=out_specs, check_vma=False
    )
```
